32 devices in a mesh: dp: 8 (over z, y), mp: 4 (over x, core).
Axes of the slice: x: 2, y: 2, z: 4, core: 2. Of those that a mesh axis runs over, the one named last changes fastest.
Arguments:
- item_table: bfloat16 [16384, 256], P('dp'), may hold values from -6 to 6
- history_owner: int32 [2048, 1], P(('dp', 'mp')), may hold values from 0 to 7; in each aligned block of 64 rows (0 to 63, 64 to 127, ...) at most 16 rows name the same one
- history_row: int32 [2048], P(('dp', 'mp')), may hold values from 0 to 2047
- w_in: bfloat16 [256, 512], replicated, may hold values from -0.375 to 0.375
- conv_a: bfloat16 [4, 3, 512, 512], P(None, None, None, 'mp'), may hold values from -0.15625 to 0.15625
- conv_b: bfloat16 [4, 3, 512, 512], P(None, None, 'mp'), may hold values from -0.15625 to 0.15625
- gains: float32 [4, 512], replicated, may hold values from 0.5 to 1.5
- w_out: bfloat16 [512, 256], replicated, may hold values from -0.25 to 0.25
- cand_row: int32 [8, 8, 8], P('dp'), may hold values from 0 to 2047
- cand_count: int32 [8, 8], P('dp'), may hold values from 1 to 8, 32 in all within a row
- pos_owner: int32 [8], P('dp'), may hold values from 0 to 7
Outputs:
- scores: float32 [8, 8, 8], P('dp')
- user_loss: float32 [8], P('dp')
The draws below stay inside these ranges and needn't reach their ends.
Inputs may be any that keep to these rules, and one draw needn't show every extreme that they name: `history_owner`: within each aligned block of 64 events no owner appears more than 16 times, and some owner appears exactly 16 times. `cand_count`: each user's counts sum to 32; the largest of them is 8.
All inputs are finite; a program needn't handle non-finite values.
Results may differ from the reference program's by a relative error of at most 0.025.
Values may be sent and summed in bfloat16 or wider, within the bound.
A program may use at most 64 MiB of HBM per device.

```python
import math
import jax
import jax.numpy as jnp
import numpy as np
from jax import lax

E = 256
C = 512
BLOCKS = 4
LEN = 256
ITEM_DEV = 2048
CPO = 8
USERS = 8
TOKENS = 2048
FETCH = 64
CAP = 16
ITEMS = 16384
NCAND = 32
N_DP = 8
N_MP = 4


def with_ends(values, key, smallest, largest):
    extent = values.shape
    index_at = [jax.random.randint(jax.random.fold_in(key, axis), (), 0, extent[axis]) for axis in range(len(extent))]
    values = values.at[tuple(index_at)].set(smallest)
    longest = extent.index(max(extent))
    index_at[longest] = (index_at[longest] + 1) % extent[longest]
    return values.at[tuple(index_at)].set(largest)


def steps_of(rng, extent, cuts, least, top_value):
    loudness, own = 1.0, jax.random.fold_in(rng, 6)
    for position, blocks in cuts:
        steps = jnp.exp(jax.random.uniform(jax.random.fold_in(own, position), (blocks,), jnp.float32, least / len(cuts), top_value / len(cuts)))
        loudness = loudness * jnp.repeat(steps, extent[position] // blocks).reshape([-1 if axis == position else 1 for axis in range(len(extent))])
    return loudness


def profile(amount, total, bound, skew):
    portions = [(1 << 20) // math.isqrt(grade ** skew) + 1 for grade in range(2, amount + 1)]
    rest, given = total - bound - (amount - 1), [1] * (amount - 1)
    while rest > 0:
        movable = [i for i in range(amount - 1) if given[i] < bound]
        pool, remaining = sum([portions[i] for i in movable]), rest
        for i in movable:
            addition = min(bound - given[i], max(1, remaining * portions[i] // pool), rest)
            given[i] = given[i] + addition
            rest = rest - addition
    return np.array([bound] + given)


def uneven_parts(own_key, amount, total, limit, skew):
    if amount == 2:
        one = jax.random.randint(own_key, (), max(1, total - limit), min(limit, total - 1) + 1)
        return jnp.stack([one, total - one])
    tallies = jnp.asarray(profile(amount, total, limit, skew), jnp.int32)
    couples = (amount - 1) // 2
    source_of, taker = tallies[1:1 + 2 * couples:2], tallies[2:2 + 2 * couples:2]
    slack = jnp.minimum(source_of - 1, limit - taker)
    passed = jax.random.randint(jax.random.fold_in(own_key, 1), (couples,), 0, 1 << 20) % (slack + 1)
    tallies = tallies.at[1:1 + 2 * couples:2].set(source_of - passed).at[2:2 + 2 * couples:2].set(taker + passed)
    return tallies[jax.random.permutation(jax.random.fold_in(own_key, 2), amount)]


def shared_out(rng, own, number, rows, count, top, limit, skew):
    sequence = jax.random.permutation(rng, count)
    crowded, usual = portions_of(count, rows * top, limit, skew, True), portions_of(count, rows * top, limit, skew, False)
    places = jnp.arange(count)

    def named(tallies, rotation):
        used = int((tallies > 0).sum())
        fixed = max(1, used // 4)
        passed = fixed + (places - fixed + rotation * (used - fixed)) % max(1, count - fixed)
        return jnp.zeros((count,), jnp.int32).at[sequence[jnp.where(places < fixed, places, passed)]].set(jnp.asarray(tallies, jnp.int32))

    tallies = jnp.where(number % 4 == 0, named(crowded, number // 4), named(usual, number - number // 4 - 1))
    mixed = jax.random.permutation(jax.random.fold_in(own, 3), count)
    giver, sink = mixed[0:count // 2 * 2:2], mixed[1:count // 2 * 2:2]
    margin = jnp.minimum(tallies[giver] - 1, limit - tallies[sink]) // 2
    margin = jnp.where((giver == sequence[0]) | (sink == sequence[0]) | (tallies[sink] == 0), 0, jnp.maximum(margin, 0))
    passed = jax.random.randint(jax.random.fold_in(own, 4), (count // 2,), 0, 1 << 20) % (margin + 1)
    tallies = tallies.at[giver].add(-passed).at[sink].add(passed)
    labels = jnp.searchsorted(jnp.cumsum(tallies), jnp.arange(rows * top), side="right").astype(jnp.int32)
    listing = labels.reshape(top, rows).T
    listing = listing[jax.random.permutation(jax.random.fold_in(own, 1), rows)]
    rotation = jax.random.randint(jax.random.fold_in(own, 2), (rows, 1), 0, top)
    return jnp.take_along_axis(listing, (jnp.arange(top)[None, :] + rotation) % top, axis=1)


def portions_of(amount, total, most, skew, full):
    weights = [(1 << 20) // math.isqrt(rank ** skew) + 1 for rank in range(1, amount + 1)]
    largest = most if full else min(most, max(-(-total // amount), total * weights[0] // sum(weights)))
    least = 1 if total - largest >= amount - 1 else 0
    given, surplus = [largest] + [least] * (amount - 1), total - largest - least * (amount - 1)
    while surplus > 0:
        movable = [i for i in range(1, amount) if given[i] < largest] or [i for i in range(1, amount) if given[i] < most]
        whole, remaining = sum([weights[i] for i in movable]), surplus
        for i in movable:
            addition = min(most - given[i], max(1, remaining * weights[i] // whole), surplus)
            given[i] = given[i] + addition
            surplus = surplus - addition
    return np.array(given)


def gaussian(own_key, dims, deviation, reach, cuts=(), kind=jnp.bfloat16):
    result = jax.random.normal(own_key, dims, jnp.float32) * deviation
    if len(cuts) > 0:
        result = steps_of(own_key, dims, cuts, -0.22, 0.18) * result
    return jnp.clip(result, min=-reach, max=reach).astype(kind)


def setup_inputs(seed: int = 0) -> dict:
    arg_keys = jax.random.split(jax.random.key(seed), 12)
    item_table = gaussian(arg_keys[0], (ITEMS, E), 1.0, 6.0, ((0, 8),))
    history_owner_keys = jax.random.split(jax.random.fold_in(arg_keys[1], 1), TOKENS // FETCH)
    history_owner_turns = jax.random.permutation(jax.random.fold_in(arg_keys[1], 3), TOKENS // FETCH)
    history_owner = jax.vmap(lambda own, number: shared_out(jax.random.fold_in(arg_keys[1], 2), own, number, FETCH, N_DP, 1, CAP, 2))(history_owner_keys, history_owner_turns).reshape((TOKENS, 1))
    history_row = with_ends(jax.random.randint(arg_keys[2], (TOKENS,), 0, ITEM_DEV), jax.random.fold_in(arg_keys[2], 1), 0, ITEM_DEV - 1).astype(jnp.int32)
    w_in = gaussian(arg_keys[3], (E, C), E ** -0.5, 0.375)
    conv_a = gaussian(arg_keys[4], (BLOCKS, 3, C, C), (3 * C) ** -0.5, 0.15625, ((3, 4),))
    conv_b = gaussian(arg_keys[5], (BLOCKS, 3, C, C), (3 * C) ** -0.5, 0.15625, ((2, 4),))
    gains = jnp.clip(1.0 + 0.1 * jax.random.normal(arg_keys[6], (BLOCKS, C), jnp.float32), 0.5, 1.5)
    w_out = gaussian(arg_keys[7], (C, E), C ** -0.5, 0.25)
    cand_row = with_ends(jax.random.randint(arg_keys[8], (USERS, N_DP, CPO), 0, ITEM_DEV), jax.random.fold_in(arg_keys[8], 1), 0, ITEM_DEV - 1).astype(jnp.int32)
    cand_count = jax.vmap(lambda own: uneven_parts(own, N_DP, NCAND, CPO, 2))(jax.random.split(arg_keys[9], USERS)).reshape((USERS, N_DP)).astype(jnp.int32)
    pos_owner = with_ends(jax.random.randint(arg_keys[10], (USERS,), 0, N_DP), jax.random.fold_in(arg_keys[10], 1), 0, N_DP - 1).astype(jnp.int32)
    return dict(item_table=item_table, history_owner=history_owner, history_row=history_row, w_in=w_in, conv_a=conv_a, conv_b=conv_b, gains=gains, w_out=w_out, cand_row=cand_row, cand_count=cand_count, pos_owner=pos_owner)


def shift_rows(values, offset):
    padded = jnp.pad(values, ((0, 0), (offset, 0), (0, 0)))
    return padded[:, :values.shape[1], :]

def causal_taps(values, dilation):
    return jnp.concatenate([values, shift_rows(values, dilation), shift_rows(values, 2 * dilation)], axis=-1)

def reference(item_table, history_owner, history_row, w_in, conv_a, conv_b, gains, w_out, cand_row, cand_count, pos_owner):
    item_ids = (history_owner[:, 0] * ITEM_DEV + history_row).astype(jnp.int32)
    embedded = item_table[item_ids]
    hidden = jnp.dot(embedded, w_in, preferred_element_type=jnp.float32).astype(jnp.bfloat16)
    hidden = hidden.reshape(USERS, LEN, C)
    quarter = C // N_MP
    for block_idx in range(BLOCKS):
        dilation = 1 if block_idx % 2 == 0 else 4
        taps_a = causal_taps(hidden, dilation).reshape(-1, 3 * C)
        rectified = jax.nn.relu(jnp.dot(taps_a, conv_a[block_idx].reshape(3 * C, C), preferred_element_type=jnp.float32)).astype(jnp.bfloat16)
        taps_b = causal_taps(rectified.reshape(USERS, LEN, C), 2 * dilation).reshape(-1, 3, C)
        branch = jnp.zeros((USERS * LEN, C), jnp.float32)
        for shard_idx in range(N_MP):
            lhs = taps_b[:, :, shard_idx * quarter:(shard_idx + 1) * quarter].reshape(-1, 3 * quarter)
            rhs = conv_b[block_idx][:, shard_idx * quarter:(shard_idx + 1) * quarter, :].reshape(3 * quarter, C)
            partial_value = jnp.dot(lhs, rhs, preferred_element_type=jnp.float32).astype(jnp.bfloat16)
            partial_value = lax.optimization_barrier(partial_value)
            branch = branch + partial_value.astype(jnp.float32)
        summed = hidden.reshape(-1, C).astype(jnp.float32) + branch
        row_mean = lax.optimization_barrier(jnp.mean(summed, axis=1, keepdims=True))
        row_msq = lax.optimization_barrier(jnp.mean(summed * summed, axis=1, keepdims=True))
        row_var = row_msq - row_mean * row_mean
        normed = (summed - row_mean) * lax.rsqrt(row_var + 1e-05) * gains[block_idx]
        hidden = normed.astype(jnp.bfloat16).reshape(USERS, LEN, C)
    last_rows = hidden[:, LEN - 1, :]
    user_vec = jnp.dot(last_rows, w_out, preferred_element_type=jnp.float32).astype(jnp.bfloat16)
    owner_base = (jnp.arange(N_DP, dtype=jnp.int32) * ITEM_DEV)[None, :, None]
    cand_rows = item_table[(owner_base + cand_row).astype(jnp.int32)]
    raw_scores = 0.25 * jnp.einsum('ue,uoce->uoc', user_vec.astype(jnp.float32), cand_rows.astype(jnp.float32))
    valid_slot = jnp.arange(CPO, dtype=jnp.int32)[None, None, :] < cand_count[:, :, None]
    scores = jnp.where(valid_slot, raw_scores, 0.0)
    exp_total = lax.optimization_barrier(jnp.sum(jnp.where(valid_slot, jnp.exp(raw_scores), 0.0), axis=(1, 2)))
    positive = jnp.take_along_axis(raw_scores[:, :, 0], pos_owner[:, None], axis=1)[:, 0]
    user_loss = jnp.log(exp_total) - positive
    return (scores, user_loss)
```

```python
import functools

import jax
import jax.numpy as jnp
from jax import lax
from jax.experimental import pallas as pl
from jax.experimental.pallas import tpu as pltpu
from jax.sharding import PartitionSpec as P

MESH = pl.DeviceIdType.MESH
DILATIONS = (1, 4, 1, 4)
F32 = jnp.float32
BF16 = jnp.bfloat16


def round_up(value, step):
    return -(-value // step) * step


def iota(shape, axis):
    return lax.broadcasted_iota(jnp.int32, shape, axis)


def rows_after(block):
    return round_up(1 + 6 * sum(DILATIONS[block + 1 :]), 16)


def kernel(
    dp, mp, capacity, cand_at, slots,
    owner_ref, row_ref, cand_ref, count_ref, pos_ref, gains_ref,
    table_hbm, w_in_hbm, conv_a_hbm, conv_b_hbm, w_out_hbm,
    scores_ref, loss_ref,
    table, w_in, conv_a, conv_b, w_out,
    message, requests, picked, arrived, parts0, parts1, parts2, parts3,
    load_sem, ask_send, ask_recv, row_send, row_recv, part_send, part_recv,
):
    user = lax.axis_index("dp")
    part = lax.axis_index("mp")
    fetch = owner_ref.shape[0]
    width = message.shape[2]
    cpo = cand_ref.shape[2]
    last = mp - 1

    loads = [
        pltpu.make_async_copy(source, target, load_sem.at[i])
        for i, (source, target) in enumerate(
            [(table_hbm, table), (w_in_hbm, w_in), (conv_a_hbm, conv_a),
             (conv_b_hbm, conv_b), (w_out_hbm, w_out)]
        )
    ]
    for load in loads:
        load.start()

    barrier = pltpu.get_barrier_semaphore()

    def greet(u, p):
        pl.semaphore_signal(barrier, inc=1, device_id=(u, p), device_id_type=MESH)

    def other_user(step):
        return lax.rem(user + step, dp)

    def other_part(step):
        return lax.rem(part + step, mp)

    def greet_same_part(step, _):
        greet(other_user(step), part)
        return 0

    def greet_askers(step, _):
        greet(other_user(step), last)
        return 0

    lax.fori_loop(1, dp, greet_same_part, 0)
    for step in range(1, mp):
        greet(user, other_part(step))

    @pl.when(part != last)
    def _():
        lax.fori_loop(1, dp, greet_askers, 0)

    @pl.when(part == last)
    def _():
        owner_col = owner_ref[...]
        square = (fetch, fetch)
        t_col, t_row = iota(square, 0), iota(square, 1)
        owner_row = jnp.sum(
            jnp.where(t_col == t_row, owner_col, 0).astype(F32), axis=0, keepdims=True
        ).astype(jnp.int32)
        before = jnp.where((owner_col == owner_row) & (t_row < t_col), 1.0, 0.0)
        rank_col = jnp.sum(before, axis=1, keepdims=True).astype(jnp.int32)
        named = jnp.where(iota((dp, fetch), 0) == owner_row, row_ref[...], 0).astype(F32)
        placed = jnp.where(iota((fetch, width), 1) == rank_col, 1.0, 0.0)
        asked = jnp.dot(
            named, placed, preferred_element_type=F32, precision=lax.Precision.HIGHEST
        )
        spread = jnp.where(iota((cpo, width), 1) == iota((cpo, width), 0) + cand_at, 1.0, 0.0)
        asked += jnp.dot(
            cand_ref[0].astype(F32), spread, preferred_element_type=F32,
            precision=lax.Precision.HIGHEST,
        )
        slot_col = owner_col * slots + rank_col
        slot_row = jnp.sum(
            jnp.where(
                iota((fetch, width), 1) == iota((fetch, width), 0) + slots, slot_col, 0
            ).astype(F32),
            axis=0, keepdims=True,
        )
        asked = (asked + slot_row + 0.5).astype(jnp.int32)
        for o in range(dp):
            message[o] = asked[o : o + 1, :]
        requests[pl.ds(user, 1)] = message[pl.ds(user, 1)]

    @pl.when(part == last)
    def _():
        pl.semaphore_wait(barrier, dp * mp - 1)

    @pl.when(part != last)
    def _():
        pl.semaphore_wait(barrier, dp - 1 + mp - 1)

    def ask(step, p):
        u = other_user(step)
        return pltpu.make_async_remote_copy(
            src_ref=message.at[u], dst_ref=requests.at[user],
            send_sem=ask_send.at[p, step], recv_sem=ask_recv.at[step],
            device_id=(u, p), device_id_type=MESH,
        )

    @pl.when(part == last)
    def _():
        def ask_all(step, _):
            for p in range(mp):
                ask(step, p).start()
            return 0

        lax.fori_loop(1, dp, ask_all, 0)
        for p in range(mp - 1):
            ask(0, p).start()

    def heard(step, _):
        ask(step, 0).wait_recv()
        return 0

    lax.fori_loop(1, dp, heard, 0)

    @pl.when(part != last)
    def _():
        heard(0, 0)

    loads[0].wait()
    group = min(dp, 8)

    def pick(index, _):
        these = pl.ds(index * group, group)
        asked = jnp.broadcast_to(requests[these], (group, slots, width))
        shape = (group, slots, width)
        column = jnp.sum(
            jnp.where(iota(shape, 1) == iota(shape, 2), asked, 0).astype(F32),
            axis=2, keepdims=True,
        ).astype(jnp.int32)
        items = table.shape[0]
        hot = jnp.where(column == iota((group, slots, items), 2), 1.0, 0.0)
        hot = hot.reshape(group * slots, items).astype(BF16)
        rows = jnp.dot(hot, table[...], preferred_element_type=F32).astype(BF16)
        picked[these] = rows.reshape(group, slots, table.shape[1])
        return 0

    lax.fori_loop(0, dp // group, pick, 0)
    arrived[pl.ds(user, 1)] = picked[pl.ds(user, 1)]

    def deliver(step):
        u = other_user(step)
        return pltpu.make_async_remote_copy(
            src_ref=picked.at[u], dst_ref=arrived.at[user],
            send_sem=row_send.at[step], recv_sem=row_recv.at[step],
            device_id=(u, part), device_id_type=MESH,
        )

    def deliver_start(step, _):
        deliver(step).start()
        return 0

    def deliver_wait(step, _):
        deliver(step).wait_recv()
        return 0

    lax.fori_loop(1, dp, deliver_start, 0)
    mine = jnp.broadcast_to(requests[user], (fetch, width))
    at = (fetch, width)
    slot_col = jnp.sum(
        jnp.where(iota(at, 1) == iota(at, 0) + slots, mine, 0).astype(F32),
        axis=1, keepdims=True,
    ).astype(jnp.int32)
    chosen = jnp.where(slot_col == iota((fetch, dp * slots), 1), 1.0, 0.0).astype(BF16)
    loads[1].wait()
    lax.fori_loop(1, dp, deliver_wait, 0)

    everything = arrived[...].reshape(dp * slots, arrived.shape[2])
    embedded = jnp.dot(chosen, everything, preferred_element_type=F32).astype(BF16)
    hidden = jnp.dot(embedded, w_in[...], preferred_element_type=F32).astype(BF16)

    loads[2].wait()
    loads[3].wait()
    loads[4].wait()
    sends = []
    for block, parts in enumerate((parts0, parts1, parts2, parts3)):
        gap = DILATIONS[block]
        keep = parts.shape[1]
        rows = hidden.shape[0]
        total = jnp.dot(hidden, conv_a[block, 0], preferred_element_type=F32)
        for tap in (1, 2):
            total += pltpu.roll(
                jnp.dot(hidden, conv_a[block, tap], preferred_element_type=F32),
                tap * gap, 0,
            )
        rectified = jnp.maximum(total, 0.0).astype(BF16).astype(F32)
        branch = jnp.dot(
            rectified[rows - keep :].astype(BF16), conv_b[block, 0], preferred_element_type=F32
        )
        for tap in (1, 2):
            branch += jnp.dot(
                pltpu.roll(rectified, tap * 2 * gap, 0)[rows - keep :].astype(BF16),
                conv_b[block, tap],
                preferred_element_type=F32,
            )
        parts[part] = branch.astype(BF16)
        copies = [
            pltpu.make_async_remote_copy(
                src_ref=parts.at[part], dst_ref=parts.at[part],
                send_sem=part_send.at[block, step], recv_sem=part_recv.at[block, step],
                device_id=(user, other_part(step)), device_id_type=MESH,
            )
            for step in range(1, mp)
        ]
        for copy in copies:
            copy.start()
        for copy in copies:
            copy.wait_recv()
        sends += copies
        added = parts[0].astype(F32)
        for p in range(1, mp):
            added += parts[p].astype(F32)
        summed = hidden[rows - keep :].astype(F32) + added
        mean = jnp.mean(summed, axis=1, keepdims=True)
        square = jnp.mean(summed * summed, axis=1, keepdims=True)
        normed = (summed - mean) * lax.rsqrt(square - mean * mean + 1e-5)
        hidden = (normed * gains_ref[block : block + 1, :]).astype(BF16)

    vectors = jnp.dot(hidden, w_out[...], preferred_element_type=F32)
    vector = vectors.astype(BF16).astype(F32)[hidden.shape[0] - 1 :, :]
    wanted = arrived[...].astype(F32)[:, cand_at : cand_at + cpo, :]
    raw = 0.25 * jnp.sum(wanted * vector[None], axis=2, keepdims=True)
    cube = (dp, cpo, cpo)
    raw = jnp.sum(jnp.where(iota(cube, 1) == iota(cube, 2), raw, 0.0), axis=1)
    count = jnp.sum(
        jnp.where(iota((dp, dp), 0) == iota((dp, dp), 1), count_ref[...], 0).astype(F32),
        axis=1, keepdims=True,
    ).astype(jnp.int32)
    slot = iota((dp, cpo), 1)
    live = slot < count
    scores_ref[0] = jnp.where(live, raw, 0.0)
    exp_total = jnp.sum(
        jnp.sum(jnp.where(live, jnp.exp(raw), 0.0), axis=1, keepdims=True), axis=0, keepdims=True
    )
    is_positive = (iota((dp, cpo), 0) == pos_ref[...]) & (slot == 0)
    positive = jnp.sum(
        jnp.sum(jnp.where(is_positive, raw, 0.0), axis=1, keepdims=True), axis=0, keepdims=True
    )
    loss_ref[...] = jnp.log(exp_total) - positive

    for copy in sends:
        copy.wait_send()

    def delivered(step, _):
        deliver(step).wait_send()
        return 0

    lax.fori_loop(1, dp, delivered, 0)

    @pl.when(part == last)
    def _():
        def asked_all(step, _):
            for p in range(mp):
                ask(step, p).wait_send()
            return 0

        lax.fori_loop(1, dp, asked_all, 0)
        for p in range(mp - 1):
            ask(0, p).wait_send()


def per_device(
    item_table, history_owner, history_row, w_in, conv_a, conv_b, gains, w_out,
    cand_row, cand_count, pos_owner,
):
    dp = lax.axis_size("dp")
    mp = lax.axis_size("mp")
    fetch = history_row.shape[0]
    embed = item_table.shape[1]
    channels = w_in.shape[1]
    cpo = cand_row.shape[2]
    capacity = max(4, 2 * fetch // dp)
    cand_at = round_up(capacity, 8)
    slots = round_up(cand_at + cpo, 16)
    width = round_up(slots + fetch, 128)
    assert cand_row.shape[0] == 1 and fetch > 6 * sum(DILATIONS)
    vmem = pl.BlockSpec(memory_space=pltpu.VMEM)
    hbm = pl.BlockSpec(memory_space=pl.ANY)
    scores, loss = pl.pallas_call(
        functools.partial(kernel, dp, mp, capacity, cand_at, slots),
        out_shape=(
            jax.ShapeDtypeStruct((1, dp, cpo), F32),
            jax.ShapeDtypeStruct((1, 1), F32),
        ),
        in_specs=[vmem] * 6 + [hbm] * 5,
        out_specs=(vmem, vmem),
        scratch_shapes=[
            pltpu.VMEM(item_table.shape, BF16),
            pltpu.VMEM(w_in.shape, BF16),
            pltpu.VMEM(conv_a.shape, BF16),
            pltpu.VMEM(conv_b.shape, BF16),
            pltpu.VMEM(w_out.shape, BF16),
            pltpu.VMEM((dp, 1, width), jnp.int32),
            pltpu.VMEM((dp, 1, width), jnp.int32),
            pltpu.VMEM((dp, slots, embed), BF16),
            pltpu.VMEM((dp, slots, embed), BF16),
        ]
        + [pltpu.VMEM((mp, rows_after(b), channels), BF16) for b in range(len(DILATIONS))]
        + [
            pltpu.SemaphoreType.DMA((5,)),
            pltpu.SemaphoreType.DMA((mp, dp)),
            pltpu.SemaphoreType.DMA((dp,)),
            pltpu.SemaphoreType.DMA((dp,)),
            pltpu.SemaphoreType.DMA((dp,)),
            pltpu.SemaphoreType.DMA((len(DILATIONS), mp)),
            pltpu.SemaphoreType.DMA((len(DILATIONS), mp)),
        ],
        compiler_params=pltpu.CompilerParams(
            collective_id=0, has_side_effects=True, vmem_limit_bytes=48 << 20
        ),
    )(
        history_owner, history_row.reshape(1, fetch), cand_row, cand_count,
        pos_owner.reshape(1, 1), gains, item_table, w_in, conv_a, conv_b, w_out,
    )
    return scores, loss.reshape(1)


def solution(mesh):
    return jax.shard_map(
        per_device,
        mesh=mesh,
        in_specs=(
            P("dp", None),
            P(("dp", "mp"), None),
            P(("dp", "mp")),
            P(),
            P(None, None, None, "mp"),
            P(None, None, "mp", None),
            P(),
            P(),
            P("dp", None, None),
            P("dp", None),
            P("dp"),
        ),
        out_specs=(P("dp", None, None), P("dp")),
        check_vma=False,
    )
```

```python
import functools

import jax
import jax.numpy as jnp
from jax import lax
from jax.experimental import pallas as pl
from jax.experimental.pallas import tpu as pltpu
from jax.sharding import PartitionSpec as P

MESH = pl.DeviceIdType.MESH
DILATIONS = (1, 4, 1, 4)
STRIDES = (1, 1, 4, 1)
F32 = jnp.float32
BF16 = jnp.bfloat16


def round_up(value, step):
    return -(-value // step) * step


def iota(shape, axis):
    return lax.broadcasted_iota(jnp.int32, shape, axis)


def rows_after(block):
    reach = 6 * sum(DILATIONS[block + 1 :]) // STRIDES[block]
    return round_up(1 + reach, 16)


def kernel(
    dp, mp, capacity, cand_at, slots,
    owner_hbm, row_hbm, cand_hbm, count_hbm, pos_hbm, gains_hbm,
    table_hbm, w_in_hbm, conv_a_hbm, conv_b_hbm, w_out_hbm,
    scores_ref, loss_ref,
    owner_ref, row_ref, cand_ref, count_ref, pos_ref, gains_ref,
    table, w_in, conv_a, conv_b, w_out,
    message, requests, picked, arrived, parts0, parts1, parts2, parts3,
    load_sem, ask_send, ask_recv, row_send, row_recv, part_send, part_recv,
):
    user = lax.axis_index("dp")
    part = lax.axis_index("mp")
    fetch = owner_ref.shape[1]
    width = message.shape[2]
    cpo = cand_ref.shape[2]
    last = mp - 1

    loads = [
        pltpu.make_async_copy(source, target, load_sem.at[i])
        for i, (source, target) in enumerate(
            [(owner_hbm, owner_ref), (row_hbm, row_ref), (cand_hbm, cand_ref),
             (table_hbm, table), (w_in_hbm, w_in), (conv_a_hbm, conv_a),
             (conv_b_hbm, conv_b), (gains_hbm, gains_ref), (w_out_hbm, w_out),
             (count_hbm, count_ref), (pos_hbm, pos_ref)]
        )
    ]
    for load in loads:
        load.start()

    barrier = pltpu.get_barrier_semaphore()

    def greet(u, p):
        pl.semaphore_signal(barrier, inc=1, device_id=(u, p), device_id_type=MESH)

    def other_user(step):
        return lax.rem(user + step, dp)

    def other_part(step):
        return lax.rem(part + step, mp)

    def greet_same_part(step, _):
        greet(other_user(step), part)
        return 0

    def greet_askers(step, _):
        greet(other_user(step), last)
        return 0

    lax.fori_loop(1, dp, greet_same_part, 0)
    for step in range(1, mp):
        greet(user, other_part(step))

    @pl.when(part != last)
    def _():
        lax.fori_loop(1, dp, greet_askers, 0)

    for load in loads[:3]:
        load.wait()

    @pl.when(part == last)
    def _():
        owner_row = owner_ref[...]
        square = (fetch, fetch)
        t_col, t_row = iota(square, 0), iota(square, 1)
        owner_col = jnp.sum(
            jnp.where(t_col == t_row, owner_row, 0).astype(F32), axis=1, keepdims=True
        ).astype(jnp.int32)
        before = jnp.where((owner_col == owner_row) & (t_row < t_col), 1.0, 0.0)
        rank_col = jnp.sum(before, axis=1, keepdims=True).astype(jnp.int32)
        named = jnp.where(iota((dp, fetch), 0) == owner_row, row_ref[...], 0).astype(F32)
        placed = jnp.where(iota((fetch, width), 1) == rank_col, 1.0, 0.0)
        asked = jnp.dot(
            named, placed, preferred_element_type=F32, precision=lax.Precision.HIGHEST
        )
        spread = jnp.where(iota((cpo, width), 1) == iota((cpo, width), 0) + cand_at, 1.0, 0.0)
        asked += jnp.dot(
            cand_ref[0].astype(F32), spread, preferred_element_type=F32,
            precision=lax.Precision.HIGHEST,
        )
        slot_col = owner_col * slots + rank_col
        slot_row = jnp.sum(
            jnp.where(
                iota((fetch, width), 1) == iota((fetch, width), 0) + slots, slot_col, 0
            ).astype(F32),
            axis=0, keepdims=True,
        )
        asked = (asked + slot_row + 0.5).astype(jnp.int32)
        for o in range(dp):
            message[o] = asked[o : o + 1, :]
        requests[pl.ds(user, 1)] = message[pl.ds(user, 1)]

    @pl.when(part == last)
    def _():
        pl.semaphore_wait(barrier, dp * mp - 1)

    @pl.when(part != last)
    def _():
        pl.semaphore_wait(barrier, dp - 1 + mp - 1)

    def ask(step, p):
        u = other_user(step)
        return pltpu.make_async_remote_copy(
            src_ref=message.at[u], dst_ref=requests.at[user],
            send_sem=ask_send.at[p, step], recv_sem=ask_recv.at[step],
            device_id=(u, p), device_id_type=MESH,
        )

    @pl.when(part == last)
    def _():
        def ask_all(step, _):
            for p in range(mp):
                ask(step, p).start()
            return 0

        lax.fori_loop(1, dp, ask_all, 0)
        for p in range(mp - 1):
            ask(0, p).start()

    def heard(step, _):
        ask(step, 0).wait_recv()
        return 0

    lax.fori_loop(1, dp, heard, 0)

    @pl.when(part != last)
    def _():
        heard(0, 0)

    loads[3].wait()
    group = min(dp, 8)

    def pick(index, _):
        these = pl.ds(index * group, group)
        asked = jnp.broadcast_to(requests[these], (group, slots, width))
        shape = (group, slots, width)
        column = jnp.sum(
            jnp.where(iota(shape, 1) == iota(shape, 2), asked, 0).astype(F32),
            axis=2, keepdims=True,
        ).astype(jnp.int32)
        items = table.shape[0]
        hot = jnp.where(column == iota((group, slots, items), 2), 1.0, 0.0)
        hot = hot.reshape(group * slots, items).astype(BF16)
        rows = jnp.dot(hot, table[...], preferred_element_type=F32).astype(BF16)
        picked[these] = rows.reshape(group, slots, table.shape[1])
        return 0

    lax.fori_loop(0, dp // group, pick, 0)
    arrived[pl.ds(user, 1)] = picked[pl.ds(user, 1)]

    def deliver(step):
        u = other_user(step)
        return pltpu.make_async_remote_copy(
            src_ref=picked.at[u], dst_ref=arrived.at[user],
            send_sem=row_send.at[step], recv_sem=row_recv.at[step],
            device_id=(u, part), device_id_type=MESH,
        )

    def deliver_start(step, _):
        deliver(step).start()
        return 0

    def deliver_wait(step, _):
        deliver(step).wait_recv()
        return 0

    lax.fori_loop(1, dp, deliver_start, 0)
    mine = jnp.broadcast_to(requests[user], (fetch, width))
    at = (fetch, width)
    slot_col = jnp.sum(
        jnp.where(iota(at, 1) == iota(at, 0) + slots, mine, 0).astype(F32),
        axis=1, keepdims=True,
    ).astype(jnp.int32)
    chosen = jnp.where(slot_col == iota((fetch, dp * slots), 1), 1.0, 0.0).astype(BF16)
    loads[4].wait()
    lax.fori_loop(1, dp, deliver_wait, 0)

    everything = arrived[...].reshape(dp * slots, arrived.shape[2])
    embedded = jnp.dot(chosen, everything, preferred_element_type=F32).astype(BF16)
    hidden = jnp.dot(embedded, w_in[...], preferred_element_type=F32).astype(BF16)

    for load in loads[5:]:
        load.wait()
    sends = []
    for block, parts in enumerate((parts0, parts1, parts2, parts3)):
        keep = parts.shape[1]
        rows = hidden.shape[0]
        stride = STRIDES[block]
        gap = DILATIONS[block] // (STRIDES[block - 1] if block else 1)
        total = jnp.dot(hidden, conv_a[block, 0], preferred_element_type=F32)
        for tap in (1, 2):
            total += pltpu.roll(
                jnp.dot(hidden, conv_a[block, tap], preferred_element_type=F32),
                tap * gap, 0,
            )
        rectified = jnp.maximum(total, 0.0).astype(BF16).astype(F32)
        branch = 0.0
        base = hidden[rows - keep :]
        if stride > 1:
            at = iota((keep, rows), 0) * stride + rows - 1 - (keep - 1) * stride
            strided = jnp.where(at == iota((keep, rows), 1), 1.0, 0.0).astype(BF16)
            base = jnp.dot(strided, hidden, preferred_element_type=F32)
        for tap in range(3):
            shifted = pltpu.roll(rectified, tap * 2 * gap, 0) if tap else rectified
            if stride > 1:
                shifted = jnp.dot(strided, shifted.astype(BF16), preferred_element_type=F32)
            else:
                shifted = shifted[rows - keep :]
            branch += jnp.dot(
                shifted.astype(BF16), conv_b[block, tap], preferred_element_type=F32
            )
        parts[part] = branch.astype(BF16)
        copies = [
            pltpu.make_async_remote_copy(
                src_ref=parts.at[part], dst_ref=parts.at[part],
                send_sem=part_send.at[block, step], recv_sem=part_recv.at[block, step],
                device_id=(user, other_part(step)), device_id_type=MESH,
            )
            for step in range(1, mp)
        ]
        for copy in copies:
            copy.start()
        for copy in copies:
            copy.wait_recv()
        sends += copies
        added = parts[0].astype(F32)
        for p in range(1, mp):
            added += parts[p].astype(F32)
        summed = base.astype(F32) + added
        mean = jnp.mean(summed, axis=1, keepdims=True)
        square = jnp.mean(summed * summed, axis=1, keepdims=True)
        normed = (summed - mean) * lax.rsqrt(square - mean * mean + 1e-5)
        hidden = (normed * gains_ref[block : block + 1, :]).astype(BF16)

    vectors = jnp.dot(hidden, w_out[...], preferred_element_type=F32)
    vector = vectors.astype(BF16).astype(F32)[hidden.shape[0] - 1 :, :]
    wanted = arrived[...].astype(F32)[:, cand_at : cand_at + cpo, :]
    raw = 0.25 * jnp.sum(wanted * vector[None], axis=2, keepdims=True)
    cube = (dp, cpo, cpo)
    raw = jnp.sum(jnp.where(iota(cube, 1) == iota(cube, 2), raw, 0.0), axis=1)
    count = jnp.sum(
        jnp.where(iota((dp, dp), 0) == iota((dp, dp), 1), count_ref[...], 0).astype(F32),
        axis=1, keepdims=True,
    ).astype(jnp.int32)
    slot = iota((dp, cpo), 1)
    live = slot < count
    scores_ref[0] = jnp.where(live, raw, 0.0)
    exp_total = jnp.sum(
        jnp.sum(jnp.where(live, jnp.exp(raw), 0.0), axis=1, keepdims=True), axis=0, keepdims=True
    )
    is_positive = (iota((dp, cpo), 0) == pos_ref[...]) & (slot == 0)
    positive = jnp.sum(
        jnp.sum(jnp.where(is_positive, raw, 0.0), axis=1, keepdims=True), axis=0, keepdims=True
    )
    loss_ref[...] = jnp.log(exp_total) - positive

    for copy in sends:
        copy.wait_send()

    def delivered(step, _):
        deliver(step).wait_send()
        return 0

    lax.fori_loop(1, dp, delivered, 0)

    @pl.when(part == last)
    def _():
        def asked_all(step, _):
            for p in range(mp):
                ask(step, p).wait_send()
            return 0

        lax.fori_loop(1, dp, asked_all, 0)
        for p in range(mp - 1):
            ask(0, p).wait_send()


def per_device(
    item_table, history_owner, history_row, w_in, conv_a, conv_b, gains, w_out,
    cand_row, cand_count, pos_owner,
):
    dp = lax.axis_size("dp")
    mp = lax.axis_size("mp")
    fetch = history_row.shape[0]
    embed = item_table.shape[1]
    channels = w_in.shape[1]
    cpo = cand_row.shape[2]
    capacity = max(4, 2 * fetch // dp)
    cand_at = round_up(capacity, 8)
    slots = round_up(cand_at + cpo, 16)
    width = round_up(slots + fetch, 128)
    assert cand_row.shape[0] == 1 and fetch > 6 * sum(DILATIONS)
    vmem = pl.BlockSpec(memory_space=pltpu.VMEM)
    hbm = pl.BlockSpec(memory_space=pl.ANY)
    scores, loss = pl.pallas_call(
        functools.partial(kernel, dp, mp, capacity, cand_at, slots),
        out_shape=(
            jax.ShapeDtypeStruct((1, dp, cpo), F32),
            jax.ShapeDtypeStruct((1, 1), F32),
        ),
        in_specs=[hbm] * 11,
        out_specs=(vmem, vmem),
        scratch_shapes=[
            pltpu.VMEM((1, fetch), jnp.int32),
            pltpu.VMEM((1, fetch), jnp.int32),
            pltpu.VMEM(cand_row.shape, jnp.int32),
            pltpu.VMEM(cand_count.shape, jnp.int32),
            pltpu.VMEM((1, 1), jnp.int32),
            pltpu.VMEM(gains.shape, F32),
            pltpu.VMEM(item_table.shape, BF16),
            pltpu.VMEM(w_in.shape, BF16),
            pltpu.VMEM(conv_a.shape, BF16),
            pltpu.VMEM(conv_b.shape, BF16),
            pltpu.VMEM(w_out.shape, BF16),
            pltpu.VMEM((dp, 1, width), jnp.int32),
            pltpu.VMEM((dp, 1, width), jnp.int32),
            pltpu.VMEM((dp, slots, embed), BF16),
            pltpu.VMEM((dp, slots, embed), BF16),
        ]
        + [pltpu.VMEM((mp, rows_after(b), channels), BF16) for b in range(len(DILATIONS))]
        + [
            pltpu.SemaphoreType.DMA((11,)),
            pltpu.SemaphoreType.DMA((mp, dp)),
            pltpu.SemaphoreType.DMA((dp,)),
            pltpu.SemaphoreType.DMA((dp,)),
            pltpu.SemaphoreType.DMA((dp,)),
            pltpu.SemaphoreType.DMA((len(DILATIONS), mp)),
            pltpu.SemaphoreType.DMA((len(DILATIONS), mp)),
        ],
        compiler_params=pltpu.CompilerParams(
            collective_id=0, has_side_effects=True, vmem_limit_bytes=60 << 20
        ),
    )(
        history_owner.reshape(1, fetch), history_row.reshape(1, fetch), cand_row, cand_count,
        pos_owner.reshape(1, 1), gains, item_table, w_in, conv_a, conv_b, w_out,
    )
    return scores, loss.reshape(1)


def solution(mesh):
    return jax.shard_map(
        per_device,
        mesh=mesh,
        in_specs=(
            P("dp", None),
            P(("dp", "mp"), None),
            P(("dp", "mp")),
            P(),
            P(None, None, None, "mp"),
            P(None, None, "mp", None),
            P(),
            P(),
            P("dp", None, None),
            P("dp", None),
            P("dp"),
        ),
        out_specs=(P("dp", None, None), P("dp")),
        check_vma=False,
    )
```

```python
import functools

import jax
import jax.numpy as jnp
from jax import lax
from jax.experimental import pallas as pl
from jax.experimental.pallas import tpu as pltpu
from jax.sharding import PartitionSpec as P

MESH = pl.DeviceIdType.MESH
DILATIONS = (1, 4, 1, 4)
STRIDES = (1, 1, 4, 1)
F32 = jnp.float32
BF16 = jnp.bfloat16


def round_up(value, step):
    return -(-value // step) * step


def iota(shape, axis):
    return lax.broadcasted_iota(jnp.int32, shape, axis)


def rows_after(block):
    reach = 6 * sum(DILATIONS[block + 1 :]) // STRIDES[block]
    return round_up(1 + reach, 16)


def kernel(
    dp, mp, cand_at, slots,
    owner_hbm, row_hbm, cand_hbm, count_hbm, pos_hbm, gains_hbm,
    table_hbm, w_in_hbm, conv_a_hbm, conv_b_hbm, w_out_hbm,
    scores_ref, loss_ref,
    owner_ref, row_ref, cand_ref, count_ref, pos_ref, gains_ref,
    table, w_in, conv_a, conv_b, w_out,
    message, requests, picked, arrived, cand_picked, cand_arrived, parts0, parts1, parts2, parts3,
    load_sem, ask_send, ask_recv, row_send, row_recv, part_send, part_recv,
):
    user = lax.axis_index("dp")
    part = lax.axis_index("mp")
    fetch = owner_ref.shape[1]
    width = message.shape[2]
    cpo = cand_ref.shape[2]
    last = mp - 1

    loads = [
        pltpu.make_async_copy(source, target, load_sem.at[i])
        for i, (source, target) in enumerate(
            [(owner_hbm, owner_ref), (row_hbm, row_ref), (cand_hbm, cand_ref),
             (table_hbm, table), (w_in_hbm, w_in), (conv_a_hbm, conv_a),
             (conv_b_hbm, conv_b), (gains_hbm, gains_ref), (w_out_hbm, w_out),
             (count_hbm, count_ref), (pos_hbm, pos_ref)]
        )
    ]
    for load in loads:
        load.start()

    barrier = pltpu.get_barrier_semaphore()

    def greet(u, p):
        pl.semaphore_signal(barrier, inc=1, device_id=(u, p), device_id_type=MESH)

    def other_user(step):
        return lax.rem(user + step, dp)

    def other_part(step):
        return lax.rem(part + step, mp)

    def greet_same_part(step, _):
        greet(other_user(step), part)
        return 0

    def greet_askers(step, _):
        greet(other_user(step), last)
        return 0

    lax.fori_loop(1, dp, greet_same_part, 0)
    for step in range(1, mp):
        greet(user, other_part(step))

    @pl.when(part != last)
    def _():
        lax.fori_loop(1, dp, greet_askers, 0)

    for load in loads[:3]:
        load.wait()

    @pl.when(part == last)
    def _():
        owner_row = owner_ref[...]
        square = (fetch, fetch)
        t_col, t_row = iota(square, 0), iota(square, 1)
        owner_col = jnp.sum(
            jnp.where(t_col == t_row, owner_row, 0).astype(F32), axis=1, keepdims=True
        ).astype(jnp.int32)
        before = jnp.where((owner_col == owner_row) & (t_row < t_col), 1.0, 0.0)
        rank_col = jnp.sum(before, axis=1, keepdims=True).astype(jnp.int32)
        named = jnp.where(iota((dp, fetch), 0) == owner_row, row_ref[...], 0).astype(F32)
        placed = jnp.where(iota((fetch, width), 1) == rank_col, 1.0, 0.0)
        asked = jnp.dot(
            named, placed, preferred_element_type=F32, precision=lax.Precision.HIGHEST
        )
        spread = jnp.where(iota((cpo, width), 1) == iota((cpo, width), 0) + cand_at, 1.0, 0.0)
        asked += jnp.dot(
            cand_ref[0].astype(F32), spread, preferred_element_type=F32,
            precision=lax.Precision.HIGHEST,
        )
        slot_col = owner_col * cand_at + rank_col
        slot_row = jnp.sum(
            jnp.where(
                iota((fetch, width), 1) == iota((fetch, width), 0) + slots, slot_col, 0
            ).astype(F32),
            axis=0, keepdims=True,
        )
        asked = (asked + slot_row + 0.5).astype(jnp.int32)
        for o in range(dp):
            message[o] = asked[o : o + 1, :]
        requests[pl.ds(user, 1)] = message[pl.ds(user, 1)]

    @pl.when(part == last)
    def _():
        pl.semaphore_wait(barrier, dp * mp - 1)

    @pl.when(part != last)
    def _():
        pl.semaphore_wait(barrier, dp - 1 + mp - 1)

    def ask(step, p):
        u = other_user(step)
        return pltpu.make_async_remote_copy(
            src_ref=message.at[u], dst_ref=requests.at[user],
            send_sem=ask_send.at[p, step], recv_sem=ask_recv.at[step],
            device_id=(u, p), device_id_type=MESH,
        )

    @pl.when(part == last)
    def _():
        def ask_all(step, _):
            for p in range(mp):
                ask(step, p).start()
            return 0

        lax.fori_loop(1, dp, ask_all, 0)
        for p in range(mp - 1):
            ask(0, p).start()

    def heard(step, _):
        ask(step, 0).wait_recv()
        return 0

    lax.fori_loop(1, dp, heard, 0)

    @pl.when(part != last)
    def _():
        heard(0, 0)

    loads[3].wait()
    group = min(dp, 8)

    def pick(first, target):
        count = target.shape[1]

        def step(index, _):
            these = pl.ds(index * group, group)
            shape = (group, count, width)
            asked = jnp.broadcast_to(requests[these], shape)
            column = jnp.sum(
                jnp.where(iota(shape, 1) + first == iota(shape, 2), asked, 0).astype(F32),
                axis=2, keepdims=True,
            ).astype(jnp.int32)
            items = table.shape[0]
            hot = jnp.where(column == iota((group, count, items), 2), 1.0, 0.0)
            hot = hot.reshape(group * count, items).astype(BF16)
            rows = jnp.dot(hot, table[...], preferred_element_type=F32).astype(BF16)
            target[these] = rows.reshape(group, count, table.shape[1])
            return 0

        if dp == group:
            step(0, 0)
        else:
            lax.fori_loop(0, dp // group, step, 0)

    def deliver(kind, step):
        source, target = ((picked, arrived), (cand_picked, cand_arrived))[kind]
        u = other_user(step)
        return pltpu.make_async_remote_copy(
            src_ref=source.at[u], dst_ref=target.at[user],
            send_sem=row_send.at[kind, step], recv_sem=row_recv.at[kind, step],
            device_id=(u, part), device_id_type=MESH,
        )

    def for_others(act):
        def body(step, _):
            act(step)
            return 0

        lax.fori_loop(1, dp, body, 0)

    pick(0, picked)
    for_others(lambda step: deliver(0, step).start())
    arrived[pl.ds(user, 1)] = picked[pl.ds(user, 1)]
    pick(cand_at, cand_picked)
    for_others(lambda step: deliver(1, step).start())
    cand_arrived[pl.ds(user, 1)] = cand_picked[pl.ds(user, 1)]
    mine = jnp.broadcast_to(requests[user], (fetch, width))
    at = (fetch, width)
    slot_col = jnp.sum(
        jnp.where(iota(at, 1) == iota(at, 0) + slots, mine, 0).astype(F32),
        axis=1, keepdims=True,
    ).astype(jnp.int32)
    chosen = jnp.where(slot_col == iota((fetch, dp * cand_at), 1), 1.0, 0.0).astype(BF16)
    loads[4].wait()
    for_others(lambda step: deliver(0, step).wait_recv())

    everything = arrived[...].reshape(dp * cand_at, arrived.shape[2])
    embedded = jnp.dot(chosen, everything, preferred_element_type=F32).astype(BF16)
    hidden = jnp.dot(embedded, w_in[...], preferred_element_type=F32).astype(BF16)

    for load in loads[5:]:
        load.wait()
    sends = []
    for block, parts in enumerate((parts0, parts1, parts2, parts3)):
        keep = parts.shape[1]
        rows = hidden.shape[0]
        stride = STRIDES[block]
        gap = DILATIONS[block] // (STRIDES[block - 1] if block else 1)
        total = jnp.dot(hidden, conv_a[block, 0], preferred_element_type=F32)
        for tap in (1, 2):
            total += pltpu.roll(
                jnp.dot(hidden, conv_a[block, tap], preferred_element_type=F32),
                tap * gap, 0,
            )
        rectified = jnp.maximum(total, 0.0).astype(BF16).astype(F32)
        branch = 0.0
        base = hidden[rows - keep :]
        if stride > 1:
            at = iota((keep, rows), 0) * stride + rows - 1 - (keep - 1) * stride
            strided = jnp.where(at == iota((keep, rows), 1), 1.0, 0.0).astype(BF16)
            base = jnp.dot(strided, hidden, preferred_element_type=F32)
        for tap in range(3):
            shifted = pltpu.roll(rectified, tap * 2 * gap, 0) if tap else rectified
            if stride > 1:
                shifted = jnp.dot(strided, shifted.astype(BF16), preferred_element_type=F32)
            else:
                shifted = shifted[rows - keep :]
            branch += jnp.dot(
                shifted.astype(BF16), conv_b[block, tap], preferred_element_type=F32
            )
        parts[part] = branch.astype(BF16)
        copies = [
            pltpu.make_async_remote_copy(
                src_ref=parts.at[part], dst_ref=parts.at[part],
                send_sem=part_send.at[block, step], recv_sem=part_recv.at[block, step],
                device_id=(user, other_part(step)), device_id_type=MESH,
            )
            for step in range(1, mp)
        ]
        for copy in copies:
            copy.start()
        for copy in copies:
            copy.wait_recv()
        sends += copies
        added = parts[0].astype(F32)
        for p in range(1, mp):
            added += parts[p].astype(F32)
        summed = base.astype(F32) + added
        mean = jnp.mean(summed, axis=1, keepdims=True)
        square = jnp.mean(summed * summed, axis=1, keepdims=True)
        normed = (summed - mean) * lax.rsqrt(square - mean * mean + 1e-5)
        hidden = (normed * gains_ref[block : block + 1, :]).astype(BF16)

    vectors = jnp.dot(hidden, w_out[...], preferred_element_type=F32)
    vector = vectors.astype(BF16).astype(F32)[hidden.shape[0] - 1 :, :]
    for_others(lambda step: deliver(1, step).wait_recv())
    wanted = cand_arrived[...].astype(F32)[:, :cpo, :]
    raw = 0.25 * jnp.sum(wanted * vector[None], axis=2, keepdims=True)
    cube = (dp, cpo, cpo)
    raw = jnp.sum(jnp.where(iota(cube, 1) == iota(cube, 2), raw, 0.0), axis=1)
    count = jnp.sum(
        jnp.where(iota((dp, dp), 0) == iota((dp, dp), 1), count_ref[...], 0).astype(F32),
        axis=1, keepdims=True,
    ).astype(jnp.int32)
    slot = iota((dp, cpo), 1)
    live = slot < count
    scores_ref[0] = jnp.where(live, raw, 0.0)
    exp_total = jnp.sum(
        jnp.sum(jnp.where(live, jnp.exp(raw), 0.0), axis=1, keepdims=True), axis=0, keepdims=True
    )
    is_positive = (iota((dp, cpo), 0) == pos_ref[0]) & (slot == 0)
    positive = jnp.sum(
        jnp.sum(jnp.where(is_positive, raw, 0.0), axis=1, keepdims=True), axis=0, keepdims=True
    )
    loss_ref[...] = jnp.log(exp_total) - positive

    for copy in sends:
        copy.wait_send()

    for_others(lambda step: deliver(0, step).wait_send())
    for_others(lambda step: deliver(1, step).wait_send())

    @pl.when(part == last)
    def _():
        def asked_all(step, _):
            for p in range(mp):
                ask(step, p).wait_send()
            return 0

        lax.fori_loop(1, dp, asked_all, 0)
        for p in range(mp - 1):
            ask(0, p).wait_send()


def per_device(
    item_table, history_owner, history_row, w_in, conv_a, conv_b, gains, w_out,
    cand_row, cand_count, pos_owner,
):
    dp = lax.axis_size("dp")
    mp = lax.axis_size("mp")
    fetch = history_row.shape[0]
    embed = item_table.shape[1]
    channels = w_in.shape[1]
    cpo = cand_row.shape[2]
    capacity = max(4, 2 * fetch // dp)
    cand_at = round_up(capacity, 16)
    cand_rows = round_up(cpo, 16)
    slots = cand_at + cand_rows
    width = round_up(slots + fetch, 128)
    assert cand_row.shape[0] == 1 and fetch > 6 * sum(DILATIONS)
    vmem = pl.BlockSpec(memory_space=pltpu.VMEM)
    hbm = pl.BlockSpec(memory_space=pl.ANY)
    scores, loss = pl.pallas_call(
        functools.partial(kernel, dp, mp, cand_at, slots),
        out_shape=(
            jax.ShapeDtypeStruct((1, dp, cpo), F32),
            jax.ShapeDtypeStruct((1, 1), F32),
        ),
        in_specs=[hbm] * 11,
        out_specs=(vmem, vmem),
        scratch_shapes=[
            pltpu.VMEM((1, fetch), jnp.int32),
            pltpu.VMEM((1, fetch), jnp.int32),
            pltpu.VMEM(cand_row.shape, jnp.int32),
            pltpu.VMEM(cand_count.shape, jnp.int32),
            pltpu.SMEM((1,), jnp.int32),
            pltpu.VMEM(gains.shape, F32),
            pltpu.VMEM(item_table.shape, BF16),
            pltpu.VMEM(w_in.shape, BF16),
            pltpu.VMEM(conv_a.shape, BF16),
            pltpu.VMEM(conv_b.shape, BF16),
            pltpu.VMEM(w_out.shape, BF16),
            pltpu.VMEM((dp, 1, width), jnp.int32),
            pltpu.VMEM((dp, 1, width), jnp.int32),
            pltpu.VMEM((dp, cand_at, embed), BF16),
            pltpu.VMEM((dp, cand_at, embed), BF16),
            pltpu.VMEM((dp, cand_rows, embed), BF16),
            pltpu.VMEM((dp, cand_rows, embed), BF16),
        ]
        + [pltpu.VMEM((mp, rows_after(b), channels), BF16) for b in range(len(DILATIONS))]
        + [
            pltpu.SemaphoreType.DMA((11,)),
            pltpu.SemaphoreType.DMA((mp, dp)),
            pltpu.SemaphoreType.DMA((dp,)),
            pltpu.SemaphoreType.DMA((2, dp)),
            pltpu.SemaphoreType.DMA((2, dp)),
            pltpu.SemaphoreType.DMA((len(DILATIONS), mp)),
            pltpu.SemaphoreType.DMA((len(DILATIONS), mp)),
        ],
        compiler_params=pltpu.CompilerParams(
            collective_id=0, has_side_effects=True, vmem_limit_bytes=60 << 20
        ),
    )(
        history_owner.reshape(1, fetch), history_row.reshape(1, fetch), cand_row, cand_count,
        pos_owner, gains, item_table, w_in, conv_a, conv_b, w_out,
    )
    return scores, loss.reshape(1)


def solution(mesh):
    return jax.shard_map(
        per_device,
        mesh=mesh,
        in_specs=(
            P("dp", None),
            P(("dp", "mp"), None),
            P(("dp", "mp")),
            P(),
            P(None, None, None, "mp"),
            P(None, None, "mp", None),
            P(),
            P(),
            P("dp", None, None),
            P("dp", None),
            P("dp"),
        ),
        out_specs=(P("dp", None, None), P("dp")),
        check_vma=False,
    )
```

```python
import functools

import jax
import jax.numpy as jnp
from jax import lax
from jax.experimental import pallas as pl
from jax.experimental.pallas import tpu as pltpu
from jax.sharding import PartitionSpec as P

MESH = pl.DeviceIdType.MESH
DILATIONS = (1, 4, 1, 4)
STRIDES = (1, 1, 4, 1)
F32 = jnp.float32
BF16 = jnp.bfloat16


def round_up(value, step):
    return -(-value // step) * step


def iota(shape, axis):
    return lax.broadcasted_iota(jnp.int32, shape, axis)


def others(dp, body):
    if dp <= 8:
        for step in range(1, dp):
            body(step, 0)
    else:
        lax.fori_loop(1, dp, body, 0)


def rows_after(block):
    reach = 6 * sum(DILATIONS[block + 1 :]) // STRIDES[block]
    return round_up(1 + reach, 16)


def kernel(
    dp, mp, cand_at, slots,
    owner_hbm, row_hbm, cand_hbm, count_hbm, pos_hbm, gains_hbm,
    table_hbm, w_in_hbm, conv_a_hbm, conv_b_hbm, w_out_hbm,
    result_ref,
    owner_ref, row_ref, cand_ref, count_ref, pos_ref, gains_ref,
    table, w_in, conv_a, conv_b, w_out,
    message, requests, picked, arrived, cand_picked, cand_arrived, parts0, parts1, parts2, parts3,
    load_sem, ask_send, ask_recv, row_send, row_recv, part_send, part_recv,
):
    user = lax.axis_index("dp")
    part = lax.axis_index("mp")
    fetch = owner_ref.shape[1]
    width = message.shape[2]
    cpo = cand_ref.shape[2]
    last = mp - 1

    loads = [
        pltpu.make_async_copy(source, target, load_sem.at[i])
        for i, (source, target) in enumerate(
            [(owner_hbm, owner_ref), (row_hbm, row_ref), (cand_hbm, cand_ref),
             (table_hbm, table), (w_in_hbm, w_in), (conv_a_hbm, conv_a),
             (conv_b_hbm, conv_b), (gains_hbm, gains_ref), (w_out_hbm, w_out),
             (count_hbm, count_ref), (pos_hbm, pos_ref)]
        )
    ]
    for load in loads:
        load.start()

    barrier = pltpu.get_barrier_semaphore()

    def greet(u, p):
        pl.semaphore_signal(barrier, inc=1, device_id=(u, p), device_id_type=MESH)

    def other_user(step):
        return lax.rem(user + step, dp)

    def other_part(step):
        return lax.rem(part + step, mp)

    def greet_same_part(step, _):
        greet(other_user(step), part)
        return 0

    def greet_askers(step, _):
        greet(other_user(step), last)
        return 0

    others(dp, greet_same_part)
    for step in range(1, mp):
        greet(user, other_part(step))

    @pl.when(part != last)
    def _():
        others(dp, greet_askers)

    for load in loads[:3]:
        load.wait()

    @pl.when(part == last)
    def _():
        owner_row = owner_ref[...]
        square = (fetch, fetch)
        t_col, t_row = iota(square, 0), iota(square, 1)
        owner_col = jnp.sum(
            jnp.where(t_col == t_row, owner_row, 0).astype(F32), axis=1, keepdims=True
        ).astype(jnp.int32)
        before = jnp.where((owner_col == owner_row) & (t_row < t_col), 1.0, 0.0)
        rank_col = jnp.sum(before, axis=1, keepdims=True).astype(jnp.int32)
        named = jnp.where(iota((dp, fetch), 0) == owner_row, row_ref[...], 0).astype(F32)
        placed = jnp.where(iota((fetch, width), 1) == rank_col, 1.0, 0.0)
        asked = jnp.dot(
            named, placed, preferred_element_type=F32, precision=lax.Precision.HIGHEST
        )
        spread = jnp.where(iota((cpo, width), 1) == iota((cpo, width), 0) + cand_at, 1.0, 0.0)
        asked += jnp.dot(
            cand_ref[0].astype(F32), spread, preferred_element_type=F32,
            precision=lax.Precision.HIGHEST,
        )
        slot_col = owner_col * cand_at + rank_col
        slot_row = jnp.sum(
            jnp.where(
                iota((fetch, width), 1) == iota((fetch, width), 0) + slots, slot_col, 0
            ).astype(F32),
            axis=0, keepdims=True,
        )
        asked = (asked + slot_row + 0.5).astype(jnp.int32)
        for o in range(dp):
            message[o] = asked[o : o + 1, :]
        requests[pl.ds(user, 1)] = message[pl.ds(user, 1)]

    @pl.when(part == last)
    def _():
        pl.semaphore_wait(barrier, dp * mp - 1)

    @pl.when(part != last)
    def _():
        pl.semaphore_wait(barrier, dp - 1 + mp - 1)

    def ask(step, p):
        u = other_user(step)
        return pltpu.make_async_remote_copy(
            src_ref=message.at[u], dst_ref=requests.at[user],
            send_sem=ask_send.at[p, step], recv_sem=ask_recv.at[step],
            device_id=(u, p), device_id_type=MESH,
        )

    @pl.when(part == last)
    def _():
        def ask_all(step, _):
            for p in range(mp):
                ask(step, p).start()
            return 0

        others(dp, ask_all)
        for p in range(mp - 1):
            ask(0, p).start()

    def heard(step, _):
        ask(step, 0).wait_recv()
        return 0

    others(dp, heard)

    @pl.when(part != last)
    def _():
        heard(0, 0)

    loads[3].wait()
    group = min(dp, 8)

    def pick(first, target):
        count = target.shape[1]

        def step(index, _):
            these = pl.ds(index * group, group)
            shape = (group, count, width)
            asked = jnp.broadcast_to(requests[these], shape)
            column = jnp.sum(
                jnp.where(iota(shape, 1) + first == iota(shape, 2), asked, 0).astype(F32),
                axis=2, keepdims=True,
            ).astype(jnp.int32)
            items = table.shape[0]
            hot = jnp.where(column == iota((group, count, items), 2), 1.0, 0.0)
            hot = hot.reshape(group * count, items).astype(BF16)
            rows = jnp.dot(hot, table[...], preferred_element_type=F32).astype(BF16)
            target[these] = rows.reshape(group, count, table.shape[1])
            return 0

        if dp == group:
            step(0, 0)
        else:
            lax.fori_loop(0, dp // group, step, 0)

    def deliver(kind, step):
        source, target = ((picked, arrived), (cand_picked, cand_arrived))[kind]
        u = other_user(step)
        return pltpu.make_async_remote_copy(
            src_ref=source.at[u], dst_ref=target.at[user],
            send_sem=row_send.at[kind, step], recv_sem=row_recv.at[kind, step],
            device_id=(u, part), device_id_type=MESH,
        )

    def for_others(act):
        def body(step, _):
            act(step)
            return 0

        others(dp, body)

    pick(0, picked)
    for_others(lambda step: deliver(0, step).start())
    arrived[pl.ds(user, 1)] = picked[pl.ds(user, 1)]
    pick(cand_at, cand_picked)
    for_others(lambda step: deliver(1, step).start())
    cand_arrived[pl.ds(user, 1)] = cand_picked[pl.ds(user, 1)]
    mine = jnp.broadcast_to(requests[user], (fetch, width))
    at = (fetch, width)
    slot_col = jnp.sum(
        jnp.where(iota(at, 1) == iota(at, 0) + slots, mine, 0).astype(F32),
        axis=1, keepdims=True,
    ).astype(jnp.int32)
    chosen = jnp.where(slot_col == iota((fetch, dp * cand_at), 1), 1.0, 0.0).astype(BF16)
    loads[4].wait()
    for_others(lambda step: deliver(0, step).wait_recv())

    everything = arrived[...].reshape(dp * cand_at, arrived.shape[2])
    embedded = jnp.dot(chosen, everything, preferred_element_type=F32).astype(BF16)
    hidden = jnp.dot(embedded, w_in[...], preferred_element_type=F32).astype(BF16)

    for load in loads[5:]:
        load.wait()
    sends = []
    for block, parts in enumerate((parts0, parts1, parts2, parts3)):
        keep = parts.shape[1]
        rows = hidden.shape[0]
        stride = STRIDES[block]
        gap = DILATIONS[block] // (STRIDES[block - 1] if block else 1)
        total = jnp.dot(hidden, conv_a[block, 0], preferred_element_type=F32)
        for tap in (1, 2):
            total += pltpu.roll(
                jnp.dot(hidden, conv_a[block, tap], preferred_element_type=F32),
                tap * gap, 0,
            )
        rectified = jnp.maximum(total, 0.0).astype(BF16).astype(F32)
        branch = 0.0
        base = hidden[rows - keep :]
        if stride > 1:
            at = iota((keep, rows), 0) * stride + rows - 1 - (keep - 1) * stride
            strided = jnp.where(at == iota((keep, rows), 1), 1.0, 0.0).astype(BF16)
            base = jnp.dot(strided, hidden, preferred_element_type=F32)
        for tap in range(3):
            shifted = pltpu.roll(rectified, tap * 2 * gap, 0) if tap else rectified
            if stride > 1:
                shifted = jnp.dot(strided, shifted.astype(BF16), preferred_element_type=F32)
            else:
                shifted = shifted[rows - keep :]
            branch += jnp.dot(
                shifted.astype(BF16), conv_b[block, tap], preferred_element_type=F32
            )
        parts[part] = branch.astype(BF16)
        copies = [
            pltpu.make_async_remote_copy(
                src_ref=parts.at[part], dst_ref=parts.at[part],
                send_sem=part_send.at[block, step], recv_sem=part_recv.at[block, step],
                device_id=(user, other_part(step)), device_id_type=MESH,
            )
            for step in range(1, mp)
        ]
        for copy in copies:
            copy.start()
        for copy in copies:
            copy.wait_recv()
        sends += copies
        added = parts[0].astype(F32)
        for p in range(1, mp):
            added += parts[p].astype(F32)
        summed = base.astype(F32) + added
        mean = jnp.mean(summed, axis=1, keepdims=True)
        square = jnp.mean(summed * summed, axis=1, keepdims=True)
        normed = (summed - mean) * lax.rsqrt(square - mean * mean + 1e-5)
        hidden = (normed * gains_ref[block : block + 1, :]).astype(BF16)

    vectors = jnp.dot(hidden, w_out[...], preferred_element_type=F32)
    vector = vectors.astype(BF16).astype(F32)[hidden.shape[0] - 1 :, :]
    for_others(lambda step: deliver(1, step).wait_recv())
    wanted = cand_arrived[...].astype(F32)[:, :cpo, :]
    raw = 0.25 * jnp.sum(wanted * vector[None], axis=2, keepdims=True)
    cube = (dp, cpo, cpo)
    raw = jnp.sum(jnp.where(iota(cube, 1) == iota(cube, 2), raw, 0.0), axis=1)
    count = jnp.sum(
        jnp.where(iota((dp, dp), 0) == iota((dp, dp), 1), count_ref[...], 0).astype(F32),
        axis=1, keepdims=True,
    ).astype(jnp.int32)
    slot = iota((dp, cpo), 1)
    live = slot < count
    scores = jnp.where(live, raw, 0.0)
    exp_total = jnp.sum(
        jnp.sum(jnp.where(live, jnp.exp(raw), 0.0), axis=1, keepdims=True), axis=0, keepdims=True
    )
    is_positive = (iota((dp, cpo), 0) == pos_ref[0]) & (slot == 0)
    positive = jnp.sum(
        jnp.sum(jnp.where(is_positive, raw, 0.0), axis=1, keepdims=True), axis=0, keepdims=True
    )
    loss = jnp.broadcast_to(jnp.log(exp_total) - positive, (dp, cpo))
    result_ref[0, :, :cpo] = scores
    result_ref[0, :, cpo:] = loss

    for copy in sends:
        copy.wait_send()

    for_others(lambda step: deliver(0, step).wait_send())
    for_others(lambda step: deliver(1, step).wait_send())

    @pl.when(part == last)
    def _():
        def asked_all(step, _):
            for p in range(mp):
                ask(step, p).wait_send()
            return 0

        others(dp, asked_all)
        for p in range(mp - 1):
            ask(0, p).wait_send()


def per_device(
    item_table, history_owner, history_row, w_in, conv_a, conv_b, gains, w_out,
    cand_row, cand_count, pos_owner,
):
    dp = lax.axis_size("dp")
    mp = lax.axis_size("mp")
    fetch = history_row.shape[0]
    embed = item_table.shape[1]
    channels = w_in.shape[1]
    cpo = cand_row.shape[2]
    capacity = max(4, 2 * fetch // dp)
    cand_at = round_up(capacity, 16)
    cand_rows = round_up(cpo, 16)
    slots = cand_at + cand_rows
    width = round_up(slots + fetch, 128)
    assert cand_row.shape[0] == 1 and fetch > 6 * sum(DILATIONS)
    vmem = pl.BlockSpec(memory_space=pltpu.VMEM)
    hbm = pl.BlockSpec(memory_space=pl.ANY)
    result = pl.pallas_call(
        functools.partial(kernel, dp, mp, cand_at, slots),
        out_shape=jax.ShapeDtypeStruct((1, dp, 2 * cpo), F32),
        in_specs=[hbm] * 11,
        out_specs=vmem,
        scratch_shapes=[
            pltpu.VMEM((1, fetch), jnp.int32),
            pltpu.VMEM((1, fetch), jnp.int32),
            pltpu.VMEM(cand_row.shape, jnp.int32),
            pltpu.VMEM(cand_count.shape, jnp.int32),
            pltpu.SMEM((1,), jnp.int32),
            pltpu.VMEM(gains.shape, F32),
            pltpu.VMEM(item_table.shape, BF16),
            pltpu.VMEM(w_in.shape, BF16),
            pltpu.VMEM(conv_a.shape, BF16),
            pltpu.VMEM(conv_b.shape, BF16),
            pltpu.VMEM(w_out.shape, BF16),
            pltpu.VMEM((dp, 1, width), jnp.int32),
            pltpu.VMEM((dp, 1, width), jnp.int32),
            pltpu.VMEM((dp, cand_at, embed), BF16),
            pltpu.VMEM((dp, cand_at, embed), BF16),
            pltpu.VMEM((dp, cand_rows, embed), BF16),
            pltpu.VMEM((dp, cand_rows, embed), BF16),
        ]
        + [pltpu.VMEM((mp, rows_after(b), channels), BF16) for b in range(len(DILATIONS))]
        + [
            pltpu.SemaphoreType.DMA((11,)),
            pltpu.SemaphoreType.DMA((mp, dp)),
            pltpu.SemaphoreType.DMA((dp,)),
            pltpu.SemaphoreType.DMA((2, dp)),
            pltpu.SemaphoreType.DMA((2, dp)),
            pltpu.SemaphoreType.DMA((len(DILATIONS), mp)),
            pltpu.SemaphoreType.DMA((len(DILATIONS), mp)),
        ],
        compiler_params=pltpu.CompilerParams(
            collective_id=0, has_side_effects=True, vmem_limit_bytes=60 << 20
        ),
    )(
        history_owner.reshape(1, fetch), history_row.reshape(1, fetch), cand_row, cand_count,
        pos_owner, gains, item_table, w_in, conv_a, conv_b, w_out,
    )
    return result[:, :, :cpo], result[:, 0, cpo]


def solution(mesh):
    return jax.shard_map(
        per_device,
        mesh=mesh,
        in_specs=(
            P("dp", None),
            P(("dp", "mp"), None),
            P(("dp", "mp")),
            P(),
            P(None, None, None, "mp"),
            P(None, None, "mp", None),
            P(),
            P(),
            P("dp", None, None),
            P("dp", None),
            P("dp"),
        ),
        out_specs=(P("dp", None, None), P("dp")),
        check_vma=False,
    )
```

```python
import functools

import jax
import jax.numpy as jnp
from jax import lax
from jax.experimental import pallas as pl
from jax.experimental.pallas import tpu as pltpu
from jax.sharding import PartitionSpec as P

MESH = pl.DeviceIdType.MESH
DILATIONS = (1, 4, 1, 4)
STRIDES = (1, 1, 4, 1)
F32 = jnp.float32
BF16 = jnp.bfloat16


def round_up(value, step):
    return -(-value // step) * step


def iota(shape, axis):
    return lax.broadcasted_iota(jnp.int32, shape, axis)


def others(dp, body):
    if dp <= 8:
        for step in sorted(range(1, dp), key=lambda step: -min(step, dp - step)):
            body(step, 0)
    else:
        lax.fori_loop(1, dp, body, 0)


def rows_after(block):
    reach = 6 * sum(DILATIONS[block + 1 :]) // STRIDES[block]
    return round_up(1 + reach, 16)


def kernel(
    dp, mp, cand_at, slots,
    owner_hbm, row_hbm, cand_hbm, count_hbm, pos_hbm, gains_hbm,
    table_hbm, w_in_hbm, conv_a_hbm, conv_b_hbm, w_out_hbm,
    result_ref,
    owner_ref, row_ref, cand_ref, count_ref, pos_ref, gains_ref,
    table, w_in, conv_a, conv_b, w_out,
    message, requests, picked, arrived, cand_picked, cand_arrived, parts0, parts1, parts2, parts3,
    load_sem, ask_send, ask_recv, row_send, row_recv, part_send, part_recv,
):
    user = lax.axis_index("dp")
    part = lax.axis_index("mp")
    fetch = owner_ref.shape[1]
    width = message.shape[2]
    cpo = cand_ref.shape[2]
    last = mp - 1

    loads = [
        pltpu.make_async_copy(source, target, load_sem.at[i])
        for i, (source, target) in enumerate(
            [(owner_hbm, owner_ref), (row_hbm, row_ref), (cand_hbm, cand_ref),
             (table_hbm, table), (w_in_hbm, w_in), (conv_a_hbm, conv_a),
             (conv_b_hbm, conv_b), (gains_hbm, gains_ref), (w_out_hbm, w_out),
             (count_hbm, count_ref), (pos_hbm, pos_ref)]
        )
    ]
    for load in loads:
        load.start()

    barrier = pltpu.get_barrier_semaphore()

    def greet(u, p):
        pl.semaphore_signal(barrier, inc=1, device_id=(u, p), device_id_type=MESH)

    def other_user(step):
        return lax.rem(user + step, dp)

    def other_part(step):
        return lax.rem(part + step, mp)

    def greet_same_part(step, _):
        greet(other_user(step), part)
        return 0

    def greet_askers(step, _):
        greet(other_user(step), last)
        return 0

    others(dp, greet_same_part)
    for step in range(1, mp):
        greet(user, other_part(step))

    @pl.when(part != last)
    def _():
        others(dp, greet_askers)

    for load in loads[:3]:
        load.wait()

    @pl.when(part == last)
    def _():
        owner_row = owner_ref[...]
        square = (fetch, fetch)
        t_col, t_row = iota(square, 0), iota(square, 1)
        owner_col = jnp.sum(
            jnp.where(t_col == t_row, owner_row, 0).astype(F32), axis=1, keepdims=True
        ).astype(jnp.int32)
        before = jnp.where((owner_col == owner_row) & (t_row < t_col), 1.0, 0.0)
        rank_col = jnp.sum(before, axis=1, keepdims=True).astype(jnp.int32)
        named = jnp.where(iota((dp, fetch), 0) == owner_row, row_ref[...], 0).astype(F32)
        placed = jnp.where(iota((fetch, width), 1) == rank_col, 1.0, 0.0)
        asked = jnp.dot(
            named, placed, preferred_element_type=F32, precision=lax.Precision.HIGHEST
        )
        spread = jnp.where(iota((cpo, width), 1) == iota((cpo, width), 0) + cand_at, 1.0, 0.0)
        asked += jnp.dot(
            cand_ref[0].astype(F32), spread, preferred_element_type=F32,
            precision=lax.Precision.HIGHEST,
        )
        slot_col = owner_col * cand_at + rank_col
        slot_row = jnp.sum(
            jnp.where(
                iota((fetch, width), 1) == iota((fetch, width), 0) + slots, slot_col, 0
            ).astype(F32),
            axis=0, keepdims=True,
        )
        asked = (asked + slot_row + 0.5).astype(jnp.int32)
        for o in range(dp):
            message[o] = asked[o : o + 1, :]
        requests[pl.ds(user, 1)] = message[pl.ds(user, 1)]

    @pl.when(part == last)
    def _():
        pl.semaphore_wait(barrier, dp * mp - 1)

    @pl.when(part != last)
    def _():
        pl.semaphore_wait(barrier, dp - 1 + mp - 1)

    def ask(step, p):
        u = other_user(step)
        return pltpu.make_async_remote_copy(
            src_ref=message.at[u], dst_ref=requests.at[user],
            send_sem=ask_send.at[p, step], recv_sem=ask_recv.at[step],
            device_id=(u, p), device_id_type=MESH,
        )

    @pl.when(part == last)
    def _():
        def ask_all(step, _):
            for p in range(mp):
                ask(step, p).start()
            return 0

        others(dp, ask_all)
        for p in range(mp - 1):
            ask(0, p).start()

    def heard(step, _):
        ask(step, 0).wait_recv()
        return 0

    others(dp, heard)

    @pl.when(part != last)
    def _():
        heard(0, 0)

    loads[3].wait()
    group = min(dp, 8)

    def pick(first, target):
        count = target.shape[1]

        def step(index, _):
            these = pl.ds(index * group, group)
            shape = (group, count, width)
            asked = jnp.broadcast_to(requests[these], shape)
            column = jnp.sum(
                jnp.where(iota(shape, 1) + first == iota(shape, 2), asked, 0).astype(F32),
                axis=2, keepdims=True,
            ).astype(jnp.int32)
            items = table.shape[0]
            hot = jnp.where(column == iota((group, count, items), 2), 1.0, 0.0)
            hot = hot.reshape(group * count, items).astype(BF16)
            rows = jnp.dot(hot, table[...], preferred_element_type=F32).astype(BF16)
            target[these] = rows.reshape(group, count, table.shape[1])
            return 0

        if dp == group:
            step(0, 0)
        else:
            lax.fori_loop(0, dp // group, step, 0)

    def deliver(kind, step):
        source, target = ((picked, arrived), (cand_picked, cand_arrived))[kind]
        u = other_user(step)
        return pltpu.make_async_remote_copy(
            src_ref=source.at[u], dst_ref=target.at[user],
            send_sem=row_send.at[kind, step], recv_sem=row_recv.at[kind, step],
            device_id=(u, part), device_id_type=MESH,
        )

    def for_others(act):
        def body(step, _):
            act(step)
            return 0

        others(dp, body)

    pick(0, picked)
    for_others(lambda step: deliver(0, step).start())
    arrived[pl.ds(user, 1)] = picked[pl.ds(user, 1)]
    pick(cand_at, cand_picked)
    for_others(lambda step: deliver(1, step).start())
    cand_arrived[pl.ds(user, 1)] = cand_picked[pl.ds(user, 1)]
    mine = jnp.broadcast_to(requests[user], (fetch, width))
    at = (fetch, width)
    slot_col = jnp.sum(
        jnp.where(iota(at, 1) == iota(at, 0) + slots, mine, 0).astype(F32),
        axis=1, keepdims=True,
    ).astype(jnp.int32)
    chosen = jnp.where(slot_col == iota((fetch, dp * cand_at), 1), 1.0, 0.0).astype(BF16)
    loads[4].wait()
    for_others(lambda step: deliver(0, step).wait_recv())

    everything = arrived[...].reshape(dp * cand_at, arrived.shape[2])
    embedded = jnp.dot(chosen, everything, preferred_element_type=F32).astype(BF16)
    hidden = jnp.dot(embedded, w_in[...], preferred_element_type=F32).astype(BF16)

    for load in loads[5:]:
        load.wait()
    sends = []
    for block, parts in enumerate((parts0, parts1, parts2, parts3)):
        keep = parts.shape[1]
        rows = hidden.shape[0]
        stride = STRIDES[block]
        gap = DILATIONS[block] // (STRIDES[block - 1] if block else 1)
        total = jnp.dot(hidden, conv_a[block, 0], preferred_element_type=F32)
        for tap in (1, 2):
            total += pltpu.roll(
                jnp.dot(hidden, conv_a[block, tap], preferred_element_type=F32),
                tap * gap, 0,
            )
        rectified = jnp.maximum(total, 0.0).astype(BF16).astype(F32)
        branch = 0.0
        base = hidden[rows - keep :]
        if stride > 1:
            at = iota((keep, rows), 0) * stride + rows - 1 - (keep - 1) * stride
            strided = jnp.where(at == iota((keep, rows), 1), 1.0, 0.0).astype(BF16)
            base = jnp.dot(strided, hidden, preferred_element_type=F32)
        for tap in range(3):
            shifted = pltpu.roll(rectified, tap * 2 * gap, 0) if tap else rectified
            if stride > 1:
                shifted = jnp.dot(strided, shifted.astype(BF16), preferred_element_type=F32)
            else:
                shifted = shifted[rows - keep :]
            branch += jnp.dot(
                shifted.astype(BF16), conv_b[block, tap], preferred_element_type=F32
            )
        parts[part] = branch.astype(BF16)
        copies = [
            pltpu.make_async_remote_copy(
                src_ref=parts.at[part], dst_ref=parts.at[part],
                send_sem=part_send.at[block, step], recv_sem=part_recv.at[block, step],
                device_id=(user, other_part(step)), device_id_type=MESH,
            )
            for step in sorted(range(1, mp), key=lambda step: -min(step, mp - step))
        ]
        for copy in copies:
            copy.start()
        for copy in copies:
            copy.wait_recv()
        sends += copies
        added = parts[0].astype(F32)
        for p in range(1, mp):
            added += parts[p].astype(F32)
        summed = base.astype(F32) + added
        mean = jnp.mean(summed, axis=1, keepdims=True)
        square = jnp.mean(summed * summed, axis=1, keepdims=True)
        normed = (summed - mean) * lax.rsqrt(square - mean * mean + 1e-5)
        hidden = (normed * gains_ref[block : block + 1, :]).astype(BF16)

    vectors = jnp.dot(hidden, w_out[...], preferred_element_type=F32)
    vector = vectors.astype(BF16).astype(F32)[hidden.shape[0] - 1 :, :]
    for_others(lambda step: deliver(1, step).wait_recv())
    wanted = cand_arrived[...].astype(F32)[:, :cpo, :]
    raw = 0.25 * jnp.sum(wanted * vector[None], axis=2, keepdims=True)
    cube = (dp, cpo, cpo)
    raw = jnp.sum(jnp.where(iota(cube, 1) == iota(cube, 2), raw, 0.0), axis=1)
    count = jnp.sum(
        jnp.where(iota((dp, dp), 0) == iota((dp, dp), 1), count_ref[...], 0).astype(F32),
        axis=1, keepdims=True,
    ).astype(jnp.int32)
    slot = iota((dp, cpo), 1)
    live = slot < count
    scores = jnp.where(live, raw, 0.0)
    exp_total = jnp.sum(
        jnp.sum(jnp.where(live, jnp.exp(raw), 0.0), axis=1, keepdims=True), axis=0, keepdims=True
    )
    is_positive = (iota((dp, cpo), 0) == pos_ref[0]) & (slot == 0)
    positive = jnp.sum(
        jnp.sum(jnp.where(is_positive, raw, 0.0), axis=1, keepdims=True), axis=0, keepdims=True
    )
    loss = jnp.broadcast_to(jnp.log(exp_total) - positive, (dp, cpo))
    result_ref[0, :, :cpo] = scores
    result_ref[0, :, cpo:] = loss

    for copy in sends:
        copy.wait_send()

    for_others(lambda step: deliver(0, step).wait_send())
    for_others(lambda step: deliver(1, step).wait_send())

    @pl.when(part == last)
    def _():
        def asked_all(step, _):
            for p in range(mp):
                ask(step, p).wait_send()
            return 0

        others(dp, asked_all)
        for p in range(mp - 1):
            ask(0, p).wait_send()


def per_device(
    item_table, history_owner, history_row, w_in, conv_a, conv_b, gains, w_out,
    cand_row, cand_count, pos_owner,
):
    dp = lax.axis_size("dp")
    mp = lax.axis_size("mp")
    fetch = history_row.shape[0]
    embed = item_table.shape[1]
    channels = w_in.shape[1]
    cpo = cand_row.shape[2]
    capacity = max(4, 2 * fetch // dp)
    cand_at = round_up(capacity, 16)
    cand_rows = round_up(cpo, 16)
    slots = cand_at + cand_rows
    width = round_up(slots + fetch, 128)
    assert cand_row.shape[0] == 1 and fetch > 6 * sum(DILATIONS)
    vmem = pl.BlockSpec(memory_space=pltpu.VMEM)
    hbm = pl.BlockSpec(memory_space=pl.ANY)
    result = pl.pallas_call(
        functools.partial(kernel, dp, mp, cand_at, slots),
        out_shape=jax.ShapeDtypeStruct((1, dp, 2 * cpo), F32),
        in_specs=[hbm] * 11,
        out_specs=vmem,
        scratch_shapes=[
            pltpu.VMEM((1, fetch), jnp.int32),
            pltpu.VMEM((1, fetch), jnp.int32),
            pltpu.VMEM(cand_row.shape, jnp.int32),
            pltpu.VMEM(cand_count.shape, jnp.int32),
            pltpu.SMEM((1,), jnp.int32),
            pltpu.VMEM(gains.shape, F32),
            pltpu.VMEM(item_table.shape, BF16),
            pltpu.VMEM(w_in.shape, BF16),
            pltpu.VMEM(conv_a.shape, BF16),
            pltpu.VMEM(conv_b.shape, BF16),
            pltpu.VMEM(w_out.shape, BF16),
            pltpu.VMEM((dp, 1, width), jnp.int32),
            pltpu.VMEM((dp, 1, width), jnp.int32),
            pltpu.VMEM((dp, cand_at, embed), BF16),
            pltpu.VMEM((dp, cand_at, embed), BF16),
            pltpu.VMEM((dp, cand_rows, embed), BF16),
            pltpu.VMEM((dp, cand_rows, embed), BF16),
        ]
        + [pltpu.VMEM((mp, rows_after(b), channels), BF16) for b in range(len(DILATIONS))]
        + [
            pltpu.SemaphoreType.DMA((11,)),
            pltpu.SemaphoreType.DMA((mp, dp)),
            pltpu.SemaphoreType.DMA((dp,)),
            pltpu.SemaphoreType.DMA((2, dp)),
            pltpu.SemaphoreType.DMA((2, dp)),
            pltpu.SemaphoreType.DMA((len(DILATIONS), mp)),
            pltpu.SemaphoreType.DMA((len(DILATIONS), mp)),
        ],
        compiler_params=pltpu.CompilerParams(
            collective_id=0, has_side_effects=True, vmem_limit_bytes=60 << 20
        ),
    )(
        history_owner.reshape(1, fetch), history_row.reshape(1, fetch), cand_row, cand_count,
        pos_owner, gains, item_table, w_in, conv_a, conv_b, w_out,
    )
    return result[:, :, :cpo], result[:, 0, cpo]


def solution(mesh):
    return jax.shard_map(
        per_device,
        mesh=mesh,
        in_specs=(
            P("dp", None),
            P(("dp", "mp"), None),
            P(("dp", "mp")),
            P(),
            P(None, None, None, "mp"),
            P(None, None, "mp", None),
            P(),
            P(),
            P("dp", None, None),
            P("dp", None),
            P("dp"),
        ),
        out_specs=(P("dp", None, None), P("dp")),
        check_vma=False,
    )
```
